32 devices in a mesh: dp: 8 (over z, core), zero: 4 (over y, x).
Axes of the slice: x: 2, y: 2, z: 4, core: 2. Of those that a mesh axis runs over, the one named last changes fastest.
Arguments:
- pre_acts: bfloat16 [4096, 2560], P(('dp', 'zero')), may hold values from -6 to 6
- cotangent: bfloat16 [4096, 640], P(('dp', 'zero')), may hold values from -6 to 6
- w_out: bfloat16 [1280, 640], P('zero'), may hold values from -0.25 to 0.25
Outputs:
- d_pre: bfloat16 [4096, 2560], P(('dp', 'zero'))
- d_w: float32 [4, 204800], P('zero', 'dp')
The draws below stay inside these ranges and needn't reach their ends.
All inputs are finite; a program needn't handle non-finite values.
Results may differ from the reference program's by a relative error of at most 0.0028.
Values may be sent and summed in bfloat16 or wider, within the bound.
A program may use at most 64 MiB of HBM per device.

```python
import math
import jax
import jax.numpy as jnp
from jax import lax

D = 640
FFH = 1280
TOKENS = 4096
N_ZERO = 4


def strengthened(array, own_key, source, target, blocks, factor):
    owner, partner = [(jnp.arange(array.shape[dim]) // (array.shape[dim] // blocks)).reshape([-1 if axis == dim else 1 for axis in range(array.ndim)]) for dim in (source, target)]
    chosen = jax.random.permutation(own_key, blocks)[partner]
    strong = (owner == chosen) | (owner == (partner + blocks // 2) % blocks)
    return jnp.where(strong, factor * array, array)


def block_scale(stream_key, dims, shards, least, largest):
    level = 1.0
    for position, blocks in shards:
        draws = jax.random.uniform(jax.random.fold_in(jax.random.fold_in(stream_key, 6), position), (blocks,), jnp.float32, least / len(shards), largest / len(shards))
        level = level * jnp.repeat(jnp.exp(draws), dims[position] // blocks).reshape((-1,) + (1,) * (len(dims) - 1 - position))
    return level


def scatter_about(key, dims, scale, most, cuts=(), dtype=jnp.bfloat16):
    drawn = jax.random.normal(key, dims, jnp.float32) * scale
    if len(cuts) > 0:
        drawn = block_scale(key, dims, cuts, -0.22, 0.18) * drawn
    return jnp.clip(drawn, min=-most, max=most).astype(dtype)


def bell_draw_with(stream_key, extent, width, reach, split, heavy, dtype=jnp.bfloat16):
    drawn = width * jax.random.normal(stream_key, extent, jnp.float32)
    if split:
        drawn = drawn * block_scale(stream_key, extent, split, -0.22, 0.18)
    return jnp.clip(strengthened(drawn, jax.random.fold_in(stream_key, 3), *heavy), -reach, reach).astype(dtype)


def setup_inputs(seed: int = 0) -> dict:
    seeds = jax.random.split(jax.random.key(seed), 4)
    return {
        "pre_acts": scatter_about(seeds[0], (TOKENS, 2 * FFH), 1.0, 6.0, ((0, 32),)),
        "cotangent": bell_draw_with(seeds[1], (TOKENS, D), 1.0, 6.0, ((0, 32),), (0, 1, 32, 2.75)),
        "w_out": scatter_about(seeds[2], (FFH, D), D ** -0.5, 0.25, ((0, 4),)),
    }


def block_grads(pre_acts, cotangent, w_out):
    value = pre_acts[:, :FFH].astype(jnp.float32)
    gate = pre_acts[:, FFH:].astype(jnp.float32)
    cdf = 0.5 * (1.0 + jax.scipy.special.erf(gate / math.sqrt(2.0)))
    act = gate * cdf
    hidden = (value * act).astype(jnp.bfloat16)
    term = jnp.dot(hidden.T, cotangent, preferred_element_type=jnp.float32)
    d_hidden = jnp.dot(cotangent, w_out.T, preferred_element_type=jnp.float32)
    dens = jnp.exp(-0.5 * gate * gate) / math.sqrt(2.0 * math.pi)
    d_value = d_hidden * act
    d_gate = d_hidden * value * (cdf + gate * dens)
    d_pre = jnp.concatenate([d_value, d_gate], axis=1).astype(jnp.bfloat16)
    return (d_pre, term)

def reference(pre_acts, cotangent, w_out):
    block = min(TOKENS, 4096)
    count = TOKENS // block
    pre_blocks = pre_acts.reshape(count, block, 2 * FFH)
    cot_blocks = cotangent.reshape(count, block, D)

    def step(carry, items):
        d_pre, term = block_grads(items[0], items[1], w_out)
        return (carry + term, d_pre)
    start = jnp.zeros((FFH, D), jnp.float32)
    total, outs = lax.scan(step, start, (pre_blocks, cot_blocks))
    d_w = (total / math.sqrt(TOKENS)).reshape(N_ZERO, FFH * D // N_ZERO)
    return (outs.reshape(TOKENS, 2 * FFH), d_w)
```

```python
import functools
import math

import jax
import jax.numpy as jnp
from jax import lax
from jax.experimental import pallas as pl
from jax.experimental.pallas import tpu as pltpu
from jax.sharding import PartitionSpec as P

LANES = 128
MESH = pl.DeviceIdType.MESH


def gate_parts(gate):
    cdf = 0.5 * (1.0 + lax.erf(gate / math.sqrt(2.0)))
    dens = jnp.exp(-0.5 * gate * gate) / math.sqrt(2.0 * math.pi)
    return gate * cdf, cdf + gate * dens


def general_body(pre_acts, cotangent, w_out):
    n_zero = lax.axis_size("zero")
    n_data = lax.axis_size("dp")
    width = cotangent.shape[1]
    ffh = pre_acts.shape[1] // 2
    scale = 1.0 / math.sqrt(pre_acts.shape[0] * n_data * n_zero)
    value = pre_acts[:, :ffh].astype(jnp.float32)
    gate = pre_acts[:, ffh:].astype(jnp.float32)
    act, slope = gate_parts(gate)
    hidden = (value * act).astype(jnp.bfloat16)
    d_hidden = jnp.einsum(
        "td,hd->th",
        cotangent,
        lax.all_gather(w_out, "zero", axis=0, tiled=True),
        preferred_element_type=jnp.float32,
    )
    d_pre = jnp.concatenate([d_hidden * act, d_hidden * value * slope], axis=1)
    d_pre = d_pre.astype(jnp.bfloat16)
    owned = lax.psum_scatter(
        jnp.einsum("th,td->hd", hidden, cotangent, preferred_element_type=jnp.float32) * scale,
        "zero",
        scatter_dimension=0,
        tiled=True,
    )
    blocks = owned.reshape(n_data, ffh // n_zero * width // n_data)
    d_w = lax.psum_scatter(blocks, "dp", scatter_dimension=0, tiled=True)
    return (d_pre, d_w)


def kernel(
    n_zero, n_data, scale,
    pre_hbm, cot_hbm, w_hbm,
    d_pre, d_w,
    pre, cot_all, w_all, act_s, slope_s, hid_t, hid_all, grad, grad_in, part, part_in,
    local_sem, cot_send, cot_recv, hid_send, hid_recv, w_send, w_recv,
    relay_send, relay_recv, pair_send, pair_recv, z_send, z_recv,
):
    tokens, width = cot_hbm.shape
    own_rows = w_hbm.shape[0]
    ffh = own_rows * n_zero
    half = own_rows // 2
    n_z = n_data // 2
    piece = own_rows // n_data
    cols = width // LANES
    zero = lax.axis_index("zero")
    dp = lax.axis_index("dp")
    core = lax.rem(dp, 2)
    z = lax.div(dp, 2)
    twin = z * 2 + (1 - core)

    def zero_at(step):
        return lax.rem(zero + step, n_zero)

    def z_at(step):
        return lax.rem(z + step, n_z)

    def rows(index, size):
        return pl.ds(pl.multiple_of(index * size, size), size)

    into = [
        pltpu.make_async_copy(cot_hbm, cot_all.at[zero], local_sem.at[0]),
        pltpu.make_async_copy(pre_hbm, pre, local_sem.at[1]),
        pltpu.make_async_copy(w_hbm, w_all.at[rows(zero, own_rows), :], local_sem.at[2]),
    ]
    for copy in into:
        copy.start()

    barrier = pltpu.get_barrier_semaphore()
    for step in range(1, n_zero):
        pl.semaphore_signal(barrier, inc=1, device_id=(dp, zero_at(step)), device_id_type=MESH)
    for step in range(1, n_z):
        pl.semaphore_signal(
            barrier, inc=1, device_id=(z_at(step) * 2 + core, zero), device_id_type=MESH
        )
    pl.semaphore_signal(barrier, inc=1, device_id=(twin, zero), device_id_type=MESH)
    pl.semaphore_wait(barrier, n_zero - 1 + n_z - 1 + 1)

    cots = []
    for step in range(1, n_zero):
        cots.append(pltpu.make_async_remote_copy(
            src_ref=cot_hbm, dst_ref=cot_all.at[zero],
            send_sem=cot_send.at[step], recv_sem=cot_recv.at[step],
            device_id=(dp, zero_at(step)), device_id_type=MESH,
        ))
        cots[-1].start()

    into[1].wait()
    for tile in range(ffh // LANES):
        at = pl.ds(tile * LANES, LANES)
        value = pre[:, at].astype(jnp.float32)
        gate = pre[:, pl.ds(ffh + tile * LANES, LANES)].astype(jnp.float32)
        act, slope = gate_parts(gate)
        act_s[:, at] = act
        slope_s[:, at] = value * slope
        hid_t[at, :] = (value * act).T.astype(jnp.bfloat16)
    hids = []
    for step in range(1, n_zero):
        hids.append(pltpu.make_async_remote_copy(
            src_ref=hid_t.at[rows(zero_at(step), own_rows), :], dst_ref=hid_all.at[zero],
            send_sem=hid_send.at[step], recv_sem=hid_recv.at[step],
            device_id=(dp, zero_at(step)), device_id_type=MESH,
        ))
        hids[-1].start()

    def w_half(block, part_of):
        return pl.ds(pl.multiple_of(block * own_rows + part_of * half, half), half)

    ws = []
    for step in range(1, n_zero):
        ws.append(pltpu.make_async_remote_copy(
            src_ref=w_hbm.at[w_half(0, core), :], dst_ref=w_all.at[w_half(zero, core), :],
            send_sem=w_send.at[step], recv_sem=w_recv.at[step],
            device_id=(dp, zero_at(step)), device_id_type=MESH,
        ))
        ws[-1].start()

    into[0].wait()
    grad[...] = jnp.dot(
        hid_t[rows(zero, own_rows), :], cot_all[zero], preferred_element_type=jnp.float32
    ).reshape(grad.shape)
    for step in range(1, n_zero):
        source = lax.rem(zero + n_zero - step, n_zero)
        cots[step - 1].wait_recv()
        hids[step - 1].wait_recv()
        grad[...] += jnp.dot(
            hid_all[source], cot_all[source], preferred_element_type=jnp.float32
        ).reshape(grad.shape)

    pairs = []
    for k in range(n_z):
        pairs.append(pltpu.make_async_remote_copy(
            src_ref=grad.at[k * 2 + (1 - core)], dst_ref=grad_in.at[k],
            send_sem=pair_send.at[k], recv_sem=pair_recv.at[k],
            device_id=(twin, zero), device_id_type=MESH,
        ))
        pairs[-1].start()

    relays = []
    for step in range(1, n_zero):
        source = lax.rem(zero + n_zero - step, n_zero)
        relays.append(pltpu.make_async_remote_copy(
            src_ref=w_all.at[w_half(source, core), :], dst_ref=w_all.at[w_half(source, core), :],
            send_sem=relay_send.at[step], recv_sem=relay_recv.at[step],
            device_id=(twin, zero), device_id_type=MESH,
        ))

    for k in range(n_z):
        pairs[k].wait_recv()
    pad = part.shape[1] - cols * piece
    sends = []
    for step in range(1, n_z):
        owner = z_at(step)
        total = (grad[owner * 2 + core] + grad_in[owner]) * scale
        tall = [total[:, i * LANES:(i + 1) * LANES] for i in range(cols)]
        if pad:
            tall.append(jnp.zeros((pad, LANES), jnp.float32))
        part[step] = jnp.concatenate(tall, axis=0).astype(jnp.bfloat16)
        sends.append(pltpu.make_async_remote_copy(
            src_ref=part.at[step], dst_ref=part_in.at[step],
            send_sem=z_send.at[step], recv_sem=z_recv.at[step],
            device_id=(owner * 2 + core, zero), device_id_type=MESH,
        ))
        sends[-1].start()

    for step in range(1, n_zero):
        ws[step - 1].wait_recv()
        relays[step - 1].start()

    into[2].wait()
    for step in range(1, n_zero):
        relays[step - 1].wait_recv()
    cot = cot_all[zero]
    for tile in range(ffh // (2 * LANES)):
        at = pl.ds(tile * 2 * LANES, 2 * LANES)
        d_hidden = lax.dot_general(
            cot, w_all[at, :], (((1,), (1,)), ((), ())), preferred_element_type=jnp.float32
        )
        d_pre[:, at] = (d_hidden * act_s[:, at]).astype(jnp.bfloat16)
        d_pre[:, pl.ds(ffh + tile * 2 * LANES, 2 * LANES)] = (
            d_hidden * slope_s[:, at]
        ).astype(jnp.bfloat16)

    d_w[...] = (grad[z * 2 + core] + grad_in[z]) * scale
    for step in range(1, n_z):
        sends[step - 1].wait_recv()
        tall = part_in[step].astype(jnp.float32)
        d_w[...] += jnp.concatenate(
            [tall[i * piece:(i + 1) * piece, :] for i in range(cols)], axis=1
        )
    for copy in cots + hids + ws + pairs + relays + sends:
        copy.wait_send()


def kernel_body(n_zero, n_data, pre_acts, cotangent, w_out):
    tokens, width = cotangent.shape
    own_rows = w_out.shape[0]
    ffh = own_rows * n_zero
    piece = own_rows // n_data
    n_z = n_data // 2
    tall = -(-(width // LANES * piece) // 16) * 16
    scale = 1.0 / math.sqrt(tokens * n_data * n_zero)
    dma = pltpu.SemaphoreType.DMA
    d_pre, d_w = pl.pallas_call(
        functools.partial(kernel, n_zero, n_data, scale),
        out_shape=(
            jax.ShapeDtypeStruct((tokens, 2 * ffh), jnp.bfloat16),
            jax.ShapeDtypeStruct((piece, width), jnp.float32),
        ),
        in_specs=[pl.BlockSpec(memory_space=pl.ANY)] * 3,
        out_specs=(pl.BlockSpec(memory_space=pltpu.VMEM),) * 2,
        scratch_shapes=[
            pltpu.VMEM((tokens, 2 * ffh), jnp.bfloat16),
            pltpu.VMEM((n_zero, tokens, width), jnp.bfloat16),
            pltpu.VMEM((ffh, width), jnp.bfloat16),
            pltpu.VMEM((tokens, ffh), jnp.float32),
            pltpu.VMEM((tokens, ffh), jnp.float32),
            pltpu.VMEM((ffh, tokens), jnp.bfloat16),
            pltpu.VMEM((n_zero, own_rows, tokens), jnp.bfloat16),
            pltpu.VMEM((n_data, piece, width), jnp.float32),
            pltpu.VMEM((n_z, piece, width), jnp.float32),
            pltpu.VMEM((n_z, tall, LANES), jnp.bfloat16),
            pltpu.VMEM((n_z, tall, LANES), jnp.bfloat16),
            dma((3,)),
            dma((n_zero,)), dma((n_zero,)),
            dma((n_zero,)), dma((n_zero,)),
            dma((n_zero,)), dma((n_zero,)),
            dma((n_zero,)), dma((n_zero,)),
            dma((n_z,)), dma((n_z,)),
            dma((n_z,)), dma((n_z,)),
        ],
        compiler_params=pltpu.CompilerParams(
            collective_id=0, has_side_effects=True, vmem_limit_bytes=40 * 1024 * 1024
        ),
    )(pre_acts, cotangent, w_out)
    return d_pre, d_w.reshape(1, piece * width)


def solution(mesh):
    n_zero, n_data = mesh.shape["zero"], mesh.shape["dp"]

    def body(pre_acts, cotangent, w_out):
        tokens, width = cotangent.shape
        own_rows = w_out.shape[0]
        fits = (
            n_zero > 1 and n_data > 2 and n_data % 2 == 0
            and own_rows % (8 * n_data) == 0 and own_rows % 32 == 0
            and width % LANES == 0 and tokens % LANES == 0
            and (own_rows * n_zero) % (2 * LANES) == 0
        )
        if not fits:
            return general_body(pre_acts, cotangent, w_out)
        return kernel_body(n_zero, n_data, pre_acts, cotangent, w_out)

    return jax.shard_map(
        body,
        mesh=mesh,
        in_specs=(P(("dp", "zero"), None), P(("dp", "zero"), None), P("zero", None)),
        out_specs=(P(("dp", "zero"), None), P("zero", "dp")),
        check_vma=False,
    )
```

```python
import functools
import math

import jax
import jax.numpy as jnp
from jax import lax
from jax.experimental import pallas as pl
from jax.experimental.pallas import tpu as pltpu
from jax.sharding import PartitionSpec as P

LANES = 128
MESH = pl.DeviceIdType.MESH


def gate_parts(gate):
    cdf = 0.5 * (1.0 + lax.erf(gate / math.sqrt(2.0)))
    dens = jnp.exp(-0.5 * gate * gate) / math.sqrt(2.0 * math.pi)
    return gate * cdf, cdf + gate * dens


def general_body(pre_acts, cotangent, w_out):
    n_zero = lax.axis_size("zero")
    n_data = lax.axis_size("dp")
    width = cotangent.shape[1]
    ffh = pre_acts.shape[1] // 2
    scale = 1.0 / math.sqrt(pre_acts.shape[0] * n_data * n_zero)
    value = pre_acts[:, :ffh].astype(jnp.float32)
    gate = pre_acts[:, ffh:].astype(jnp.float32)
    act, slope = gate_parts(gate)
    hidden = (value * act).astype(jnp.bfloat16)
    d_hidden = jnp.einsum(
        "td,hd->th",
        cotangent,
        lax.all_gather(w_out, "zero", axis=0, tiled=True),
        preferred_element_type=jnp.float32,
    )
    d_pre = jnp.concatenate([d_hidden * act, d_hidden * value * slope], axis=1)
    d_pre = d_pre.astype(jnp.bfloat16)
    owned = lax.psum_scatter(
        jnp.einsum("th,td->hd", hidden, cotangent, preferred_element_type=jnp.float32) * scale,
        "zero",
        scatter_dimension=0,
        tiled=True,
    )
    blocks = owned.reshape(n_data, ffh // n_zero * width // n_data)
    d_w = lax.psum_scatter(blocks, "dp", scatter_dimension=0, tiled=True)
    return (d_pre, d_w)


def kernel(
    n_zero, n_data, scale,
    pre_hbm, cot_hbm, w_hbm,
    d_pre, d_w,
    pre, cot_all, w_all, act_s, slope_s, hid_t, hid_all, grad, grad_in, part, part_in,
    local_sem, cot_send, cot_recv, hid_send, hid_recv, w_send, w_recv,
    relay_send, relay_recv, pair_send, pair_recv, z_send, z_recv,
):
    tokens, width = cot_hbm.shape
    own_rows = w_hbm.shape[0]
    ffh = own_rows * n_zero
    n_z = n_data // 2
    piece = own_rows // n_data
    cols = width // LANES
    zero = lax.axis_index("zero")
    dp = lax.axis_index("dp")
    core = lax.rem(dp, 2)
    z = lax.div(dp, 2)
    twin = z * 2 + (1 - core)
    a = zero + 1 - 2 * lax.rem(zero, 2)
    b = lax.rem(zero + 2, 4)
    c = lax.rem(a + 2, 4)

    def z_at(step):
        return lax.rem(z + step, n_z)

    def rows(index, size):
        return pl.ds(pl.multiple_of(index * size, size), size)

    def remote(src, dst, sems, i, group, data=dp):
        return pltpu.make_async_remote_copy(
            src_ref=src, dst_ref=dst, send_sem=sems[0].at[i], recv_sem=sems[1].at[i],
            device_id=(data, group), device_id_type=MESH,
        )

    into = [
        pltpu.make_async_copy(cot_hbm, cot_all.at[zero], local_sem.at[0]),
        pltpu.make_async_copy(pre_hbm, pre, local_sem.at[1]),
        pltpu.make_async_copy(w_hbm, w_all.at[rows(zero, own_rows), :], local_sem.at[2]),
    ]
    for copy in into:
        copy.start()

    barrier = pltpu.get_barrier_semaphore()
    for peer in (a, b, c):
        pl.semaphore_signal(barrier, inc=1, device_id=(dp, peer), device_id_type=MESH)
    for step in range(1, n_z):
        pl.semaphore_signal(
            barrier, inc=1, device_id=(z_at(step) * 2 + core, zero), device_id_type=MESH
        )
    pl.semaphore_signal(barrier, inc=1, device_id=(twin, zero), device_id_type=MESH)
    pl.semaphore_wait(barrier, 3 + n_z - 1 + 1)

    upper, lower = pl.ds(0, tokens // 2), pl.ds(tokens // 2, tokens // 2)
    sems = (cot_send, cot_recv)

    def cot_at(peer, part_of):
        return cot_all.at[peer, part_of, :]

    cots = [
        remote(cot_hbm.at[upper, :], cot_at(zero, upper), sems, 0, a),
        remote(cot_hbm.at[lower, :], cot_at(zero, lower), sems, 1, b),
        remote(cot_hbm.at[lower, :], cot_at(zero, lower), sems, 2, a),
        remote(cot_hbm.at[upper, :], cot_at(zero, upper), sems, 3, b),
        remote(cot_at(a, upper), cot_at(a, upper), sems, 4, b),
        remote(cot_at(b, lower), cot_at(b, lower), sems, 5, a),
    ]
    for copy in cots[:4]:
        copy.start()

    into[1].wait()
    for tile in range(ffh // LANES):
        at = pl.ds(tile * LANES, LANES)
        value = pre[:, at].astype(jnp.float32)
        gate = pre[:, pl.ds(ffh + tile * LANES, LANES)].astype(jnp.float32)
        act, slope = gate_parts(gate)
        act_s[:, at] = act
        slope_s[:, at] = value * slope
        hid_t[at, :] = (value * act).T.astype(jnp.bfloat16)
    hids = [
        remote(hid_t.at[rows(peer, own_rows), :], hid_all.at[zero], (hid_send, hid_recv), i, peer)
        for i, peer in enumerate((c, a, b))
    ]
    for copy in hids:
        copy.start()
    cots[0].wait_recv()
    cots[4].start()
    cots[1].wait_recv()
    cots[5].start()

    quarter = own_rows // 4
    sems = (w_send, w_recv)

    def w_quarter(ref, block, q):
        at = block * own_rows + core * (2 * quarter) + q * quarter
        return ref.at[pl.ds(pl.multiple_of(at, quarter), quarter), :]

    ws = [
        remote(w_quarter(w_hbm, 0, 0), w_quarter(w_all, zero, 0), sems, 0, a),
        remote(w_quarter(w_hbm, 0, 1), w_quarter(w_all, zero, 1), sems, 1, b),
        remote(w_quarter(w_hbm, 0, 1), w_quarter(w_all, zero, 1), sems, 2, a),
        remote(w_quarter(w_hbm, 0, 0), w_quarter(w_all, zero, 0), sems, 3, b),
        remote(w_quarter(w_all, a, 0), w_quarter(w_all, a, 0), sems, 4, b),
        remote(w_quarter(w_all, b, 1), w_quarter(w_all, b, 1), sems, 5, a),
    ]
    for copy in ws[:4]:
        copy.start()

    into[0].wait()
    grad[...] = jnp.dot(
        hid_t[rows(zero, own_rows), :], cot_all[zero], preferred_element_type=jnp.float32
    ).reshape(grad.shape)
    for hid, halves, source in (
        (hids[1], (cots[2],), a), (hids[2], (cots[3],), b), (hids[0], (cots[4], cots[5]), c)
    ):
        hid.wait_recv()
        for copy in halves:
            copy.wait_recv()
        grad[...] += jnp.dot(
            hid_all[source], cot_all[source], preferred_element_type=jnp.float32
        ).reshape(grad.shape)

    pairs = [
        remote(grad.at[k * 2 + (1 - core)], grad_in.at[k], (pair_send, pair_recv), k, zero, twin)
        for k in range(n_z)
    ]
    for copy in pairs:
        copy.start()
    ws[0].wait_recv()
    ws[4].start()
    ws[1].wait_recv()
    ws[5].start()

    for copy in pairs:
        copy.wait_recv()
    pad = part.shape[1] - cols * piece
    sends = []
    for step in range(1, n_z):
        owner = z_at(step)
        total = (grad[owner * 2 + core] + grad_in[owner]) * scale
        tall = [total[:, i * LANES:(i + 1) * LANES] for i in range(cols)]
        if pad:
            tall.append(jnp.zeros((pad, LANES), jnp.float32))
        part[step] = jnp.concatenate(tall, axis=0).astype(jnp.bfloat16)
        sends.append(remote(
            part.at[step], part_in.at[step], (z_send, z_recv), step, zero, owner * 2 + core
        ))
        sends[-1].start()

    def w_half(block):
        at = pl.ds(pl.multiple_of(block * own_rows + core * (2 * quarter), quarter), 2 * quarter)
        return w_all.at[at, :]

    relays = []
    for i, (source, halves) in enumerate((
        (a, (ws[2],)), (b, (ws[3],)), (c, (ws[4], ws[5]))
    )):
        for copy in halves:
            copy.wait_recv()
        relays.append(
            remote(w_half(source), w_half(source), (relay_send, relay_recv), i, zero, twin)
        )
        relays[-1].start()

    into[2].wait()
    for copy in relays:
        copy.wait_recv()
    cot = cot_all[zero]
    for tile in range(ffh // (2 * LANES)):
        at = pl.ds(tile * 2 * LANES, 2 * LANES)
        d_hidden = lax.dot_general(
            cot, w_all[at, :], (((1,), (1,)), ((), ())), preferred_element_type=jnp.float32
        )
        d_pre[:, at] = (d_hidden * act_s[:, at]).astype(jnp.bfloat16)
        d_pre[:, pl.ds(ffh + tile * 2 * LANES, 2 * LANES)] = (
            d_hidden * slope_s[:, at]
        ).astype(jnp.bfloat16)

    d_w[...] = (grad[z * 2 + core] + grad_in[z]) * scale
    for step in range(1, n_z):
        sends[step - 1].wait_recv()
        tall = part_in[step].astype(jnp.float32)
        d_w[...] += jnp.concatenate(
            [tall[i * piece:(i + 1) * piece, :] for i in range(cols)], axis=1
        )
    for copy in cots + hids + ws + pairs + relays + sends:
        copy.wait_send()


def kernel_body(n_zero, n_data, pre_acts, cotangent, w_out):
    tokens, width = cotangent.shape
    own_rows = w_out.shape[0]
    ffh = own_rows * n_zero
    piece = own_rows // n_data
    n_z = n_data // 2
    tall = -(-(width // LANES * piece) // 16) * 16
    scale = 1.0 / math.sqrt(tokens * n_data * n_zero)
    dma = pltpu.SemaphoreType.DMA
    d_pre, d_w = pl.pallas_call(
        functools.partial(kernel, n_zero, n_data, scale),
        out_shape=(
            jax.ShapeDtypeStruct((tokens, 2 * ffh), jnp.bfloat16),
            jax.ShapeDtypeStruct((piece, width), jnp.float32),
        ),
        in_specs=[pl.BlockSpec(memory_space=pl.ANY)] * 3,
        out_specs=(pl.BlockSpec(memory_space=pltpu.VMEM),) * 2,
        scratch_shapes=[
            pltpu.VMEM((tokens, 2 * ffh), jnp.bfloat16),
            pltpu.VMEM((n_zero, tokens, width), jnp.bfloat16),
            pltpu.VMEM((ffh, width), jnp.bfloat16),
            pltpu.VMEM((tokens, ffh), jnp.float32),
            pltpu.VMEM((tokens, ffh), jnp.float32),
            pltpu.VMEM((ffh, tokens), jnp.bfloat16),
            pltpu.VMEM((n_zero, own_rows, tokens), jnp.bfloat16),
            pltpu.VMEM((n_data, piece, width), jnp.float32),
            pltpu.VMEM((n_z, piece, width), jnp.float32),
            pltpu.VMEM((n_z, tall, LANES), jnp.bfloat16),
            pltpu.VMEM((n_z, tall, LANES), jnp.bfloat16),
            dma((3,)),
            dma((6,)), dma((6,)),
            dma((3,)), dma((3,)),
            dma((6,)), dma((6,)),
            dma((3,)), dma((3,)),
            dma((n_z,)), dma((n_z,)),
            dma((n_z,)), dma((n_z,)),
        ],
        compiler_params=pltpu.CompilerParams(
            collective_id=0, has_side_effects=True, vmem_limit_bytes=60 * 1024 * 1024
        ),
    )(pre_acts, cotangent, w_out)
    return d_pre, d_w.reshape(1, piece * width)


def solution(mesh):
    n_zero, n_data = mesh.shape["zero"], mesh.shape["dp"]

    def body(pre_acts, cotangent, w_out):
        tokens, width = cotangent.shape
        own_rows = w_out.shape[0]
        fits = (
            n_zero == 4 and n_data > 2 and n_data % 2 == 0
            and own_rows % (8 * n_data) == 0 and own_rows % 64 == 0
            and width % LANES == 0 and tokens % LANES == 0
            and (own_rows * n_zero) % (2 * LANES) == 0
        )
        if not fits:
            return general_body(pre_acts, cotangent, w_out)
        return kernel_body(n_zero, n_data, pre_acts, cotangent, w_out)

    return jax.shard_map(
        body,
        mesh=mesh,
        in_specs=(P(("dp", "zero"), None), P(("dp", "zero"), None), P("zero", None)),
        out_specs=(P(("dp", "zero"), None), P("zero", "dp")),
        check_vma=False,
    )
```

```python
import functools
import math

import jax
import jax.numpy as jnp
from jax import lax
from jax.experimental import pallas as pl
from jax.experimental.pallas import tpu as pltpu
from jax.sharding import PartitionSpec as P

LANES = 128
MESH = pl.DeviceIdType.MESH


def gate_parts(gate):
    cdf = 0.5 * (1.0 + lax.erf(gate / math.sqrt(2.0)))
    dens = jnp.exp(-0.5 * gate * gate) / math.sqrt(2.0 * math.pi)
    return gate * cdf, cdf + gate * dens


def general_body(pre_acts, cotangent, w_out):
    n_zero = lax.axis_size("zero")
    n_data = lax.axis_size("dp")
    width = cotangent.shape[1]
    ffh = pre_acts.shape[1] // 2
    scale = 1.0 / math.sqrt(pre_acts.shape[0] * n_data * n_zero)
    value = pre_acts[:, :ffh].astype(jnp.float32)
    gate = pre_acts[:, ffh:].astype(jnp.float32)
    act, slope = gate_parts(gate)
    hidden = (value * act).astype(jnp.bfloat16)
    d_hidden = jnp.einsum(
        "td,hd->th",
        cotangent,
        lax.all_gather(w_out, "zero", axis=0, tiled=True),
        preferred_element_type=jnp.float32,
    )
    d_pre = jnp.concatenate([d_hidden * act, d_hidden * value * slope], axis=1)
    d_pre = d_pre.astype(jnp.bfloat16)
    owned = lax.psum_scatter(
        jnp.einsum("th,td->hd", hidden, cotangent, preferred_element_type=jnp.float32) * scale,
        "zero",
        scatter_dimension=0,
        tiled=True,
    )
    blocks = owned.reshape(n_data, ffh // n_zero * width // n_data)
    d_w = lax.psum_scatter(blocks, "dp", scatter_dimension=0, tiled=True)
    return (d_pre, d_w)


def kernel(
    n_zero, n_data, scale,
    pre_hbm, cot_hbm, w_hbm,
    d_pre, d_w,
    pre, cot_all, w_all, act_s, slope_s, hid_t, hid_all, grad, grad_in, part, part_in,
    local_sem, cot_send, cot_recv, hid_send, hid_recv, w_send, w_recv,
    relay_send, relay_recv, pair_send, pair_recv, z_send, z_recv,
):
    tokens, width = cot_hbm.shape
    own_rows = w_hbm.shape[0]
    ffh = own_rows * n_zero
    n_z = n_data // 2
    piece = own_rows // n_data
    cols = width // LANES
    zero = lax.axis_index("zero")
    dp = lax.axis_index("dp")
    core = lax.rem(dp, 2)
    z = lax.div(dp, 2)
    twin = z * 2 + (1 - core)
    a = zero + 1 - 2 * lax.rem(zero, 2)
    b = lax.rem(zero + 2, 4)
    c = lax.rem(a + 2, 4)

    def z_at(step):
        return lax.rem(z + step, n_z)

    def rows(index, size):
        return pl.ds(pl.multiple_of(index * size, size), size)

    def remote(src, dst, sems, i, group, data=dp):
        return pltpu.make_async_remote_copy(
            src_ref=src, dst_ref=dst, send_sem=sems[0].at[i], recv_sem=sems[1].at[i],
            device_id=(data, group), device_id_type=MESH,
        )

    into = [
        pltpu.make_async_copy(cot_hbm, cot_all.at[zero], local_sem.at[0]),
        pltpu.make_async_copy(pre_hbm, pre, local_sem.at[1]),
        pltpu.make_async_copy(w_hbm, w_all.at[rows(zero, own_rows), :], local_sem.at[2]),
    ]
    for copy in into:
        copy.start()

    barrier = pltpu.get_barrier_semaphore()
    for peer in (a, b, c):
        pl.semaphore_signal(barrier, inc=1, device_id=(dp, peer), device_id_type=MESH)
    for step in range(1, n_z):
        pl.semaphore_signal(
            barrier, inc=1, device_id=(z_at(step) * 2 + core, zero), device_id_type=MESH
        )
    pl.semaphore_signal(barrier, inc=1, device_id=(twin, zero), device_id_type=MESH)
    pl.semaphore_wait(barrier, 3 + n_z - 1 + 1)

    upper, lower = pl.ds(0, tokens // 2), pl.ds(tokens // 2, tokens // 2)
    sems = (cot_send, cot_recv)

    def cot_at(peer, part_of):
        return cot_all.at[peer, part_of, :]

    cots = [
        remote(cot_hbm.at[upper, :], cot_at(zero, upper), sems, 0, a),
        remote(cot_hbm.at[lower, :], cot_at(zero, lower), sems, 1, b),
        remote(cot_hbm.at[lower, :], cot_at(zero, lower), sems, 2, a),
        remote(cot_hbm.at[upper, :], cot_at(zero, upper), sems, 3, b),
        remote(cot_at(a, upper), cot_at(a, upper), sems, 4, b),
        remote(cot_at(b, lower), cot_at(b, lower), sems, 5, a),
    ]
    for copy in cots[:4]:
        copy.start()

    into[1].wait()
    for tile in range(ffh // LANES):
        at = pl.ds(tile * LANES, LANES)
        value = pre[:, at].astype(jnp.float32)
        gate = pre[:, pl.ds(ffh + tile * LANES, LANES)].astype(jnp.float32)
        act, slope = gate_parts(gate)
        act_s[:, at] = act
        slope_s[:, at] = value * slope
        hid_t[at, :] = (value * act).T.astype(jnp.bfloat16)
    hids = [
        remote(hid_t.at[rows(peer, own_rows), :], hid_all.at[zero], (hid_send, hid_recv), i, peer)
        for i, peer in enumerate((c, a, b))
    ]
    for copy in hids:
        copy.start()
    cots[0].wait_recv()
    cots[4].start()
    cots[1].wait_recv()
    cots[5].start()

    quarter = own_rows // 4
    sems = (w_send, w_recv)

    def w_quarter(ref, block, q):
        at = block * own_rows + core * (2 * quarter) + q * quarter
        return ref.at[pl.ds(pl.multiple_of(at, quarter), quarter), :]

    ws = [
        remote(w_quarter(w_hbm, 0, 0), w_quarter(w_all, zero, 0), sems, 0, a),
        remote(w_quarter(w_hbm, 0, 1), w_quarter(w_all, zero, 1), sems, 1, b),
        remote(w_quarter(w_hbm, 0, 1), w_quarter(w_all, zero, 1), sems, 2, a),
        remote(w_quarter(w_hbm, 0, 0), w_quarter(w_all, zero, 0), sems, 3, b),
        remote(w_quarter(w_all, a, 0), w_quarter(w_all, a, 0), sems, 4, b),
        remote(w_quarter(w_all, b, 1), w_quarter(w_all, b, 1), sems, 5, a),
    ]
    for copy in ws[:4]:
        copy.start()

    into[0].wait()
    grad[...] = jnp.dot(
        hid_t[rows(zero, own_rows), :], cot_all[zero], preferred_element_type=jnp.float32
    ).reshape(grad.shape)
    for hid, halves, source in (
        (hids[1], (cots[2],), a), (hids[2], (cots[3],), b), (hids[0], (cots[4], cots[5]), c)
    ):
        hid.wait_recv()
        for copy in halves:
            copy.wait_recv()
        grad[...] += jnp.dot(
            hid_all[source], cot_all[source], preferred_element_type=jnp.float32
        ).reshape(grad.shape)

    pairs = [
        remote(grad.at[k * 2 + (1 - core)], grad_in.at[k], (pair_send, pair_recv), k, zero, twin)
        for k in range(n_z)
    ]
    for copy in pairs:
        copy.start()
    ws[0].wait_recv()
    ws[4].start()
    ws[1].wait_recv()
    ws[5].start()

    for copy in pairs:
        copy.wait_recv()
    pad = part.shape[1] - cols * piece
    sends = []
    for step in range(1, n_z):
        owner = z_at(step)
        total = (grad[owner * 2 + core] + grad_in[owner]) * scale
        tall = [total[:, i * LANES:(i + 1) * LANES] for i in range(cols)]
        if pad:
            tall.append(jnp.zeros((pad, LANES), jnp.float32))
        part[step] = jnp.concatenate(tall, axis=0).astype(jnp.bfloat16)
        sends.append(remote(
            part.at[step], part_in.at[step], (z_send, z_recv), step, zero, owner * 2 + core
        ))
        sends[-1].start()

    def w_half(block):
        at = pl.ds(pl.multiple_of(block * own_rows + core * (2 * quarter), quarter), 2 * quarter)
        return w_all.at[at, :]

    relays = []
    for i, (source, halves) in enumerate((
        (a, (ws[2],)), (b, (ws[3],)), (c, (ws[4], ws[5]))
    )):
        for copy in halves:
            copy.wait_recv()
        relays.append(
            remote(w_half(source), w_half(source), (relay_send, relay_recv), i, zero, twin)
        )
        relays[-1].start()

    into[2].wait()
    for copy in relays:
        copy.wait_recv()
    cot = cot_all[zero]
    for tile in range(ffh // (2 * LANES)):
        at = pl.ds(tile * 2 * LANES, 2 * LANES)
        d_hidden = lax.dot_general(
            cot, w_all[at, :], (((1,), (1,)), ((), ())), preferred_element_type=jnp.float32
        )
        d_pre[:, at] = (d_hidden * act_s[:, at]).astype(jnp.bfloat16)
        d_pre[:, pl.ds(ffh + tile * 2 * LANES, 2 * LANES)] = (
            d_hidden * slope_s[:, at]
        ).astype(jnp.bfloat16)

    d_w[...] = (grad[z * 2 + core] + grad_in[z]) * scale
    for step in range(1, n_z):
        sends[step - 1].wait_recv()
        tall = part_in[step].astype(jnp.float32)
        d_w[...] += jnp.concatenate(
            [tall[i * piece:(i + 1) * piece, :] for i in range(cols)], axis=1
        )
    for copy in cots + hids + ws + pairs + relays + sends:
        copy.wait_send()


def kernel_body(n_zero, n_data, pre_acts, cotangent, w_out):
    tokens, width = cotangent.shape
    own_rows = w_out.shape[0]
    ffh = own_rows * n_zero
    piece = own_rows // n_data
    n_z = n_data // 2
    tall = -(-(width // LANES * piece) // 16) * 16
    scale = 1.0 / math.sqrt(tokens * n_data * n_zero)
    dma = pltpu.SemaphoreType.DMA
    pre_acts, cotangent, w_out = (
        pltpu.with_memory_space_constraint(x, pltpu.HBM) for x in (pre_acts, cotangent, w_out)
    )
    d_pre, d_w = pl.pallas_call(
        functools.partial(kernel, n_zero, n_data, scale),
        out_shape=(
            jax.ShapeDtypeStruct((tokens, 2 * ffh), jnp.bfloat16),
            jax.ShapeDtypeStruct((piece, width), jnp.float32),
        ),
        in_specs=[pl.BlockSpec(memory_space=pl.ANY)] * 3,
        out_specs=(pl.BlockSpec(memory_space=pltpu.VMEM),) * 2,
        scratch_shapes=[
            pltpu.VMEM((tokens, 2 * ffh), jnp.bfloat16),
            pltpu.VMEM((n_zero, tokens, width), jnp.bfloat16),
            pltpu.VMEM((ffh, width), jnp.bfloat16),
            pltpu.VMEM((tokens, ffh), jnp.float32),
            pltpu.VMEM((tokens, ffh), jnp.float32),
            pltpu.VMEM((ffh, tokens), jnp.bfloat16),
            pltpu.VMEM((n_zero, own_rows, tokens), jnp.bfloat16),
            pltpu.VMEM((n_data, piece, width), jnp.float32),
            pltpu.VMEM((n_z, piece, width), jnp.float32),
            pltpu.VMEM((n_z, tall, LANES), jnp.bfloat16),
            pltpu.VMEM((n_z, tall, LANES), jnp.bfloat16),
            dma((3,)),
            dma((6,)), dma((6,)),
            dma((3,)), dma((3,)),
            dma((6,)), dma((6,)),
            dma((3,)), dma((3,)),
            dma((n_z,)), dma((n_z,)),
            dma((n_z,)), dma((n_z,)),
        ],
        compiler_params=pltpu.CompilerParams(
            collective_id=0, has_side_effects=True, vmem_limit_bytes=40 * 1024 * 1024
        ),
    )(pre_acts, cotangent, w_out)
    return d_pre, d_w.reshape(1, piece * width)


def solution(mesh):
    n_zero, n_data = mesh.shape["zero"], mesh.shape["dp"]

    def body(pre_acts, cotangent, w_out):
        tokens, width = cotangent.shape
        own_rows = w_out.shape[0]
        fits = (
            n_zero == 4 and n_data > 2 and n_data % 2 == 0
            and own_rows % (8 * n_data) == 0 and own_rows % 64 == 0
            and width % LANES == 0 and tokens % LANES == 0
            and (own_rows * n_zero) % (2 * LANES) == 0
        )
        if not fits:
            return general_body(pre_acts, cotangent, w_out)
        return kernel_body(n_zero, n_data, pre_acts, cotangent, w_out)

    return jax.shard_map(
        body,
        mesh=mesh,
        in_specs=(P(("dp", "zero"), None), P(("dp", "zero"), None), P("zero", None)),
        out_specs=(P(("dp", "zero"), None), P("zero", "dp")),
        check_vma=False,
    )
```

```python
import functools
import math

import jax
import jax.numpy as jnp
from jax import lax
from jax.experimental import pallas as pl
from jax.experimental.pallas import tpu as pltpu
from jax.sharding import PartitionSpec as P

LANES = 128
MESH = pl.DeviceIdType.MESH


def gate_parts(gate):
    cdf = 0.5 * (1.0 + lax.erf(gate / math.sqrt(2.0)))
    dens = jnp.exp(-0.5 * gate * gate) / math.sqrt(2.0 * math.pi)
    return gate * cdf, cdf + gate * dens


def general_body(pre_acts, cotangent, w_out):
    n_zero = lax.axis_size("zero")
    n_data = lax.axis_size("dp")
    width = cotangent.shape[1]
    ffh = pre_acts.shape[1] // 2
    scale = 1.0 / math.sqrt(pre_acts.shape[0] * n_data * n_zero)
    value = pre_acts[:, :ffh].astype(jnp.float32)
    gate = pre_acts[:, ffh:].astype(jnp.float32)
    act, slope = gate_parts(gate)
    hidden = (value * act).astype(jnp.bfloat16)
    d_hidden = jnp.einsum(
        "td,hd->th",
        cotangent,
        lax.all_gather(w_out, "zero", axis=0, tiled=True),
        preferred_element_type=jnp.float32,
    )
    d_pre = jnp.concatenate([d_hidden * act, d_hidden * value * slope], axis=1)
    d_pre = d_pre.astype(jnp.bfloat16)
    owned = lax.psum_scatter(
        jnp.einsum("th,td->hd", hidden, cotangent, preferred_element_type=jnp.float32) * scale,
        "zero",
        scatter_dimension=0,
        tiled=True,
    )
    blocks = owned.reshape(n_data, ffh // n_zero * width // n_data)
    d_w = lax.psum_scatter(blocks, "dp", scatter_dimension=0, tiled=True)
    return (d_pre, d_w)


def kernel(
    n_zero, n_data, scale,
    pre_hbm, cot_hbm, w_hbm,
    d_pre, d_w,
    pre, cot_all, w_all, act_s, slope_s, hid_t, hid_all, grad, grad_in, part, part_in,
    local_sem, cot_send, cot_recv, hid_send, hid_recv, w_send, w_recv,
    relay_send, relay_recv, pair_send, pair_recv, z_send, z_recv,
):
    tokens, width = cot_hbm.shape
    own_rows = w_hbm.shape[0]
    ffh = own_rows * n_zero
    n_z = n_data // 2
    piece = own_rows // n_data
    cols = width // LANES
    zero = lax.axis_index("zero")
    dp = lax.axis_index("dp")
    core = lax.rem(dp, 2)
    z = lax.div(dp, 2)
    twin = z * 2 + (1 - core)
    a = zero + 1 - 2 * lax.rem(zero, 2)
    b = lax.rem(zero + 2, 4)
    c = lax.rem(a + 2, 4)

    def z_at(step):
        return lax.rem(z + step, n_z)

    def rows(index, size):
        return pl.ds(pl.multiple_of(index * size, size), size)

    def remote(src, dst, sems, i, group, data=dp):
        return pltpu.make_async_remote_copy(
            src_ref=src, dst_ref=dst, send_sem=sems[0].at[i], recv_sem=sems[1].at[i],
            device_id=(data, group), device_id_type=MESH,
        )

    into = [
        pltpu.make_async_copy(cot_hbm, cot_all.at[zero], local_sem.at[0]),
        pltpu.make_async_copy(pre_hbm, pre, local_sem.at[1]),
        pltpu.make_async_copy(w_hbm, w_all.at[rows(zero, own_rows), :], local_sem.at[2]),
    ]
    for copy in into:
        copy.start()

    barrier = pltpu.get_barrier_semaphore()
    for peer in (a, b, c):
        pl.semaphore_signal(barrier, inc=1, device_id=(dp, peer), device_id_type=MESH)
    for step in range(1, n_z):
        pl.semaphore_signal(
            barrier, inc=1, device_id=(z_at(step) * 2 + core, zero), device_id_type=MESH
        )
    pl.semaphore_signal(barrier, inc=1, device_id=(twin, zero), device_id_type=MESH)
    into[1].wait()
    for tile in range(ffh // LANES):
        at = pl.ds(tile * LANES, LANES)
        value = pre[:, at].astype(jnp.float32)
        gate = pre[:, pl.ds(ffh + tile * LANES, LANES)].astype(jnp.float32)
        act, slope = gate_parts(gate)
        act_s[:, at] = act
        slope_s[:, at] = value * slope
        hid_t[at, :] = (value * act).T.astype(jnp.bfloat16)
    pl.semaphore_wait(barrier, 3 + n_z - 1 + 1)

    upper, lower = pl.ds(0, tokens // 2), pl.ds(tokens // 2, tokens // 2)
    sems = (cot_send, cot_recv)

    def cot_at(peer, part_of):
        return cot_all.at[peer, part_of, :]

    cots = [
        remote(cot_hbm.at[upper, :], cot_at(zero, upper), sems, 0, a),
        remote(cot_hbm.at[lower, :], cot_at(zero, lower), sems, 1, b),
        remote(cot_hbm.at[lower, :], cot_at(zero, lower), sems, 2, a),
        remote(cot_hbm.at[upper, :], cot_at(zero, upper), sems, 3, b),
        remote(cot_at(a, upper), cot_at(a, upper), sems, 4, b),
        remote(cot_at(b, lower), cot_at(b, lower), sems, 5, a),
    ]
    for copy in cots[:4]:
        copy.start()

    hids = [
        remote(hid_t.at[rows(peer, own_rows), :], hid_all.at[zero], (hid_send, hid_recv), i, peer)
        for i, peer in enumerate((c, a, b))
    ]
    for copy in hids:
        copy.start()
    cots[0].wait_recv()
    cots[4].start()
    cots[1].wait_recv()
    cots[5].start()

    quarter = own_rows // 4
    sems = (w_send, w_recv)

    def w_quarter(ref, block, q):
        at = block * own_rows + core * (2 * quarter) + q * quarter
        return ref.at[pl.ds(pl.multiple_of(at, quarter), quarter), :]

    ws = [
        remote(w_quarter(w_hbm, 0, 0), w_quarter(w_all, zero, 0), sems, 0, a),
        remote(w_quarter(w_hbm, 0, 1), w_quarter(w_all, zero, 1), sems, 1, b),
        remote(w_quarter(w_hbm, 0, 1), w_quarter(w_all, zero, 1), sems, 2, a),
        remote(w_quarter(w_hbm, 0, 0), w_quarter(w_all, zero, 0), sems, 3, b),
        remote(w_quarter(w_all, a, 0), w_quarter(w_all, a, 0), sems, 4, b),
        remote(w_quarter(w_all, b, 1), w_quarter(w_all, b, 1), sems, 5, a),
    ]
    for copy in ws[:4]:
        copy.start()

    into[0].wait()
    grad[...] = jnp.dot(
        hid_t[rows(zero, own_rows), :], cot_all[zero], preferred_element_type=jnp.float32
    ).reshape(grad.shape)
    for hid, halves, source in (
        (hids[1], (cots[2],), a), (hids[2], (cots[3],), b), (hids[0], (cots[4], cots[5]), c)
    ):
        hid.wait_recv()
        for copy in halves:
            copy.wait_recv()
        grad[...] += jnp.dot(
            hid_all[source], cot_all[source], preferred_element_type=jnp.float32
        ).reshape(grad.shape)

    pairs = [
        remote(grad.at[k * 2 + (1 - core)], grad_in.at[k], (pair_send, pair_recv), k, zero, twin)
        for k in range(n_z)
    ]
    for copy in pairs:
        copy.start()
    ws[0].wait_recv()
    ws[4].start()
    ws[1].wait_recv()
    ws[5].start()

    for copy in pairs:
        copy.wait_recv()
    pad = part.shape[1] - cols * piece
    sends = []
    for step in range(1, n_z):
        owner = z_at(step)
        total = (grad[owner * 2 + core] + grad_in[owner]) * scale
        tall = [total[:, i * LANES:(i + 1) * LANES] for i in range(cols)]
        if pad:
            tall.append(jnp.zeros((pad, LANES), jnp.float32))
        part[step] = jnp.concatenate(tall, axis=0).astype(jnp.bfloat16)
        sends.append(remote(
            part.at[step], part_in.at[step], (z_send, z_recv), step, zero, owner * 2 + core
        ))
        sends[-1].start()

    def w_half(block):
        at = pl.ds(pl.multiple_of(block * own_rows + core * (2 * quarter), quarter), 2 * quarter)
        return w_all.at[at, :]

    relays = []
    for i, (source, halves) in enumerate((
        (a, (ws[2],)), (b, (ws[3],)), (c, (ws[4], ws[5]))
    )):
        for copy in halves:
            copy.wait_recv()
        relays.append(
            remote(w_half(source), w_half(source), (relay_send, relay_recv), i, zero, twin)
        )
        relays[-1].start()

    into[2].wait()
    for copy in relays:
        copy.wait_recv()
    cot = cot_all[zero]
    for tile in range(ffh // (2 * LANES)):
        at = pl.ds(tile * 2 * LANES, 2 * LANES)
        d_hidden = lax.dot_general(
            cot, w_all[at, :], (((1,), (1,)), ((), ())), preferred_element_type=jnp.float32
        )
        d_pre[:, at] = (d_hidden * act_s[:, at]).astype(jnp.bfloat16)
        d_pre[:, pl.ds(ffh + tile * 2 * LANES, 2 * LANES)] = (
            d_hidden * slope_s[:, at]
        ).astype(jnp.bfloat16)

    total = (grad[z * 2 + core] + grad_in[z]) * scale
    for step in range(1, n_z):
        sends[step - 1].wait_recv()
        tall = part_in[step].astype(jnp.float32)
        total += jnp.concatenate(
            [tall[i * piece:(i + 1) * piece, :] for i in range(cols)], axis=1
        )
    for row in range(piece):
        d_w[:, pl.ds(row * width, width)] = total[row:row + 1, :]
    for copy in cots + hids + ws + pairs + relays + sends:
        copy.wait_send()


def kernel_body(n_zero, n_data, pre_acts, cotangent, w_out):
    tokens, width = cotangent.shape
    own_rows = w_out.shape[0]
    ffh = own_rows * n_zero
    piece = own_rows // n_data
    n_z = n_data // 2
    tall = -(-(width // LANES * piece) // 16) * 16
    scale = 1.0 / math.sqrt(tokens * n_data * n_zero)
    dma = pltpu.SemaphoreType.DMA
    pre_acts, cotangent, w_out = (
        pltpu.with_memory_space_constraint(x, pltpu.HBM) for x in (pre_acts, cotangent, w_out)
    )
    d_pre, d_w = pl.pallas_call(
        functools.partial(kernel, n_zero, n_data, scale),
        out_shape=(
            jax.ShapeDtypeStruct((tokens, 2 * ffh), jnp.bfloat16),
            jax.ShapeDtypeStruct((1, piece * width), jnp.float32),
        ),
        in_specs=[pl.BlockSpec(memory_space=pl.ANY)] * 3,
        out_specs=(pl.BlockSpec(memory_space=pltpu.VMEM),) * 2,
        scratch_shapes=[
            pltpu.VMEM((tokens, 2 * ffh), jnp.bfloat16),
            pltpu.VMEM((n_zero, tokens, width), jnp.bfloat16),
            pltpu.VMEM((ffh, width), jnp.bfloat16),
            pltpu.VMEM((tokens, ffh), jnp.float32),
            pltpu.VMEM((tokens, ffh), jnp.float32),
            pltpu.VMEM((ffh, tokens), jnp.bfloat16),
            pltpu.VMEM((n_zero, own_rows, tokens), jnp.bfloat16),
            pltpu.VMEM((n_data, piece, width), jnp.float32),
            pltpu.VMEM((n_z, piece, width), jnp.float32),
            pltpu.VMEM((n_z, tall, LANES), jnp.bfloat16),
            pltpu.VMEM((n_z, tall, LANES), jnp.bfloat16),
            dma((3,)),
            dma((6,)), dma((6,)),
            dma((3,)), dma((3,)),
            dma((6,)), dma((6,)),
            dma((3,)), dma((3,)),
            dma((n_z,)), dma((n_z,)),
            dma((n_z,)), dma((n_z,)),
        ],
        compiler_params=pltpu.CompilerParams(
            collective_id=0, has_side_effects=True, vmem_limit_bytes=40 * 1024 * 1024
        ),
    )(pre_acts, cotangent, w_out)
    return d_pre, d_w


def solution(mesh):
    n_zero, n_data = mesh.shape["zero"], mesh.shape["dp"]

    def body(pre_acts, cotangent, w_out):
        tokens, width = cotangent.shape
        own_rows = w_out.shape[0]
        fits = (
            n_zero == 4 and n_data > 2 and n_data % 2 == 0
            and own_rows % (8 * n_data) == 0 and own_rows % 64 == 0
            and width % LANES == 0 and tokens % LANES == 0
            and (own_rows * n_zero) % (2 * LANES) == 0
        )
        if not fits:
            return general_body(pre_acts, cotangent, w_out)
        return kernel_body(n_zero, n_data, pre_acts, cotangent, w_out)

    return jax.shard_map(
        body,
        mesh=mesh,
        in_specs=(P(("dp", "zero"), None), P(("dp", "zero"), None), P("zero", None)),
        out_specs=(P(("dp", "zero"), None), P("zero", "dp")),
        check_vma=False,
    )
```
